32 devices in a mesh: batch: 2 (over x), row: 16 (over z, y, core).
Axes of the slice: x: 2, y: 2, z: 4, core: 2. Of those that a mesh axis runs over, the one named last changes fastest.
Arguments:
- pred_points: float32 [8, 16384], P(None, ('batch', 'row')), parts along dimension 1, may hold values from 0 to 1
- obs_points: float32 [8, 16384], P(None, ('batch', 'row')), parts along dimension 1, may hold values from 0 to 1
- predicted: float32 [16, 16384], P(None, ('batch', 'row')), parts along dimension 1, may hold values from 0.2 to 5
- observed: float32 [16, 16384], P(None, ('batch', 'row')), parts along dimension 1, may hold values from 0.2 to 5
Outputs:
- log_u: float32 [16, 16384], P(None, ('batch', 'row')), parts along dimension 1
- log_v: float32 [16, 16384], P(None, ('batch', 'row')), parts along dimension 1
The draws below stay inside these ranges and needn't reach their ends.
There are 2 independent parts, one for each index of `batch`. The reference program is written for one: setup_inputs(seed, part) draws one part's arguments, and reference() takes and returns one part's arrays. A program takes and returns all parts, laid end to end along the dimension named above; each array names one. Nothing has to cross between parts.
All inputs are finite; a program needn't handle non-finite values.
Results may differ from the reference program's by a relative error of at most 0.00055.
Values may be sent and summed in bfloat16 or wider, within the bound.
A program may use at most 64 MiB of HBM per device.

```python
import math
import jax
import jax.numpy as jnp
from jax import lax

FREQS = 16
COORDS = 8
ITERS = 3
TOTAL = 8192


def steps_of(key, extent, pieces, least, high):
    def one(axis_at, shards_of):
        heights = jax.random.uniform(jax.random.fold_in(jax.random.fold_in(key, 6), axis_at), (shards_of,), jnp.float32, least / len(pieces), high / len(pieces))
        return jnp.repeat(jnp.exp(heights), extent[axis_at] // shards_of).reshape((-1,) + (1,) * (len(extent) - axis_at - 1))

    factor_of = one(*pieces[0])
    for cut in pieces[1:]:
        factor_of = factor_of * one(*cut)
    return factor_of


def setup_inputs(seed: int = 0, part: int = 0) -> dict:
    arg_keys = jax.random.split(jax.random.key(seed), 5)
    own_keys = jax.random.split(jax.random.fold_in(arg_keys[4], part), 5)
    return {
        "pred_points": jnp.clip(1.0 * jax.random.uniform(own_keys[0], (COORDS, TOTAL), jnp.float32) ** steps_of(own_keys[0], (COORDS, TOTAL), ((1, 16),), -0.2, 0.2), 0.0, 1.0),
        "obs_points": jnp.clip(1.0 * jax.random.uniform(own_keys[1], (COORDS, TOTAL), jnp.float32) ** steps_of(own_keys[1], (COORDS, TOTAL), ((1, 16),), -0.2, 0.2), 0.0, 1.0),
        "predicted": jnp.clip(jnp.exp(math.log(5.0) - 3.218876 * jax.random.uniform(own_keys[2], (FREQS, TOTAL), jnp.float32) ** steps_of(own_keys[2], (FREQS, TOTAL), ((1, 16),), -0.2, 0.2)), 0.2, 5.0),
        "observed": jnp.clip(jnp.exp(math.log(5.0) - 3.218876 * jax.random.uniform(own_keys[3], (FREQS, TOTAL), jnp.float32) ** steps_of(own_keys[3], (FREQS, TOTAL), ((1, 16),), -0.2, 0.2)), 0.2, 5.0),
    }


ENTROPY = 0.1


def kernel_block(source_pts, target_pts):
    squared = jnp.zeros((source_pts.shape[1], target_pts.shape[1]), jnp.float32)
    for coord in range(source_pts.shape[0]):
        gap = source_pts[coord][:, None] - target_pts[coord][None, :]
        squared = squared + gap * gap
    return jnp.exp(-squared / ENTROPY).astype(jnp.bfloat16)


def contract_last(vectors, block):
    return lax.dot_general(vectors, block, (((1,), (1,)), ((), ())), preferred_element_type=jnp.float32)


def reference(pred_points, obs_points, predicted, observed):
    point_count = pred_points.shape[1]
    block_rows = math.gcd(point_count, 1024)
    block_starts = jnp.arange(point_count // block_rows, dtype=jnp.int32) * block_rows

    def row_block(first_row):
        return kernel_block(lax.dynamic_slice_in_dim(pred_points, first_row, block_rows, 1), obs_points)

    def block_sums(first_row):
        return jnp.sum(row_block(first_row).astype(jnp.float32), axis=1)

    def row_products(vectors):
        def one_block(first_row):
            return contract_last(vectors, row_block(first_row))
        stacked = lax.map(one_block, block_starts)
        return jnp.moveaxis(stacked, 0, 1).reshape(vectors.shape[0], point_count)

    def column_products(weights):
        def add_block(running, first_row):
            chosen = lax.dynamic_slice_in_dim(weights, first_row, block_rows, 1)
            return running + jnp.dot(chosen, row_block(first_row), preferred_element_type=jnp.float32), None
        result, unused = lax.scan(add_block, jnp.zeros(weights.shape, jnp.float32), block_starts)
        return result

    row_sums = lax.map(block_sums, block_starts).reshape(point_count)
    scale_u = predicted / row_sums[None, :]
    scale_v = observed
    for iteration in range(ITERS):
        if iteration > 0:
            scale_u = predicted / row_products(scale_v.astype(jnp.bfloat16))
        scale_v = observed / column_products(scale_u.astype(jnp.bfloat16))
    return jnp.log(scale_u), jnp.log(scale_v)
```

```python
import functools

import jax
import jax.numpy as jnp
from jax import lax
from jax.experimental import pallas as pl
from jax.experimental.pallas import tpu as pltpu
from jax.sharding import PartitionSpec as P

ITERS = 3
ENTROPY = 0.1
DEPTH = 64


def xor_index(left, right, bits):
    total = 0
    for bit in range(bits):
        unit = 1 << bit
        total = total + unit * ((left // unit + right // unit) % 2)
    return total


def three_parts(value):
    first = value.astype(jnp.bfloat16).astype(jnp.float32)
    rest = value - first
    second = rest.astype(jnp.bfloat16).astype(jnp.float32)
    return first, second, rest - second


def operand(points, is_source):
    centred = points - 0.5
    norm = jnp.sum(centred * centred, axis=0, keepdims=True) * (-1.0 / ENTROPY)
    n1, n2, n3 = three_parts(jnp.broadcast_to(norm, points.shape))
    row = lax.broadcasted_iota(jnp.int32, points.shape, 0)
    one, zero = jnp.ones_like(points), jnp.zeros_like(points)
    if is_source:
        a1, a2, a3 = three_parts(centred * (2.0 / ENTROPY))
        pieces = [a1, a1, a2, a2, a1, a3]
        n_first, one_first = 0, 3
    else:
        b1, b2, b3 = three_parts(centred)
        pieces = [b1, b2, b1, b2, b3, b1]
        n_first, one_first = 3, 0
    norms = jnp.where((row >= one_first) & (row < one_first + 3), one, zero)
    for place, part in enumerate((n1, n2, n3)):
        norms = jnp.where(row == n_first + place, part, norms)
    return jnp.concatenate(pieces + [norms, zero], axis=0)


def kernel(
    chips, pred_ref, obs_ref, predicted_ref, observed_ref, u_ref, v_ref,
    obs_buf, pred_buf, predicted_buf, source, cells, acc, weights,
    col_send, col_recv, v_send, v_recv, row_send, row_recv,
    obs_sems, col_sems, v_sems, sib_sems,
):
    points = pred_ref.shape[1]
    freqs = predicted_ref.shape[0]
    me = lax.axis_index("row")
    core, chip = me % 2, me // 2
    sibling = {"row": me + 1 - 2 * core}
    bits = chips.bit_length() - 1
    power = chips == 1 << bits

    def ahead(step):
        other = xor_index(chip, step, bits) if power else (chip + step) % chips
        return {"row": other * 2 + core}

    def behind(step):
        other = xor_index(chip, step, bits) if power else (chip + chips - step) % chips
        return {"row": other * 2 + core}

    def remote(src, dst, sems, place, target):
        return pltpu.make_async_remote_copy(
            src_ref=src, dst_ref=dst, send_sem=sems.at[(0, *place)], recv_sem=sems.at[(1, *place)],
            device_id=target, device_id_type=pl.DeviceIdType.MESH,
        )

    def obs_copy(step):
        return remote(obs_ref, obs_buf.at[step], obs_sems, (step,), ahead(step))

    def col_copy(k, step):
        return remote(col_send.at[k, step], col_recv.at[k, step], col_sems, (k, step), behind(step))

    def v_copy(k, step):
        return remote(v_send.at[k], v_recv.at[k, step], v_sems, (k, step), ahead(step))

    def row_copy(k):
        return remote(row_send.at[k], row_recv.at[k], sib_sems, (2 + k,), sibling)

    pred_copy = remote(pred_ref, pred_buf, sib_sems, (0,), sibling)
    predicted_copy = remote(predicted_ref, predicted_buf, sib_sems, (1,), sibling)

    def each(first, last, act):
        lax.fori_loop(first, last, lambda at, _: (act(at), 0)[1], 0)

    barrier = pltpu.get_barrier_semaphore()
    pl.semaphore_signal(barrier, inc=1, device_id=sibling, device_id_type=pl.DeviceIdType.MESH)
    each(1, chips, lambda step: pl.semaphore_signal(
        barrier, inc=1, device_id=ahead(step), device_id_type=pl.DeviceIdType.MESH))
    obs_buf[0] = obs_ref[...]
    acc[...] = jnp.zeros_like(acc)
    source[:points] = operand(pred_ref[...], True).T.astype(jnp.bfloat16)
    pl.semaphore_wait(barrier, chips)

    pred_copy.start()
    each(1, chips, lambda at: obs_copy(chips - at).start())
    predicted_copy.start()
    pred_copy.wait_recv()
    source[points:] = operand(pred_buf[...], True).T.astype(jnp.bfloat16)

    tile = min(256, points)

    def build(step):
        @pl.when(step > 0)
        def _():
            obs_copy(step).wait_recv()

        target = operand(obs_buf[step], False).astype(jnp.bfloat16)
        for first in range(0, 2 * points, tile):
            rows = slice(first, first + tile)
            exponent = jnp.dot(source[rows], target, preferred_element_type=jnp.float32)
            block = jnp.exp(exponent).astype(jnp.bfloat16)
            cells[step, rows] = block
            wide = block.astype(jnp.float32)
            sums = acc[rows]
            for lane in range(0, points, 128):
                sums = sums + wide[:, lane:lane + 128]
            acc[rows] = sums

    each(0, chips, build)
    row_sums = jnp.sum(acc[...].T, axis=0, keepdims=True)
    row_send[0] = jnp.broadcast_to(row_sums, row_send.shape[1:])
    row_copy(0).start()
    predicted_copy.wait_recv()

    for k in range(ITERS):
        if k > 0:
            @pl.when(chips > 1)
            def _():
                each(1, chips, lambda at: v_copy(k - 1, chips - at).start())

            def add_rows(step, total):
                @pl.when(step > 0)
                def _():
                    v_copy(k - 1, step).wait_recv()

                return total + lax.dot_general(
                    v_recv[k - 1, step], cells[step], (((1,), (1,)), ((), ())),
                    preferred_element_type=jnp.float32,
                )

            row_send[k] = lax.fori_loop(
                0, chips, add_rows, jnp.zeros((freqs, 2 * points), jnp.float32))
            row_copy(k).start()
        row_copy(k).wait_recv()
        own = predicted_ref[...] / (row_send[k, :, :points] + row_recv[k, :, points:])
        other = predicted_buf[...] / (row_send[k, :, points:] + row_recv[k, :, :points])
        weights[:, :points] = own.astype(jnp.bfloat16)
        weights[:, points:] = other.astype(jnp.bfloat16)
        if k == ITERS - 1:
            u_ref[...] = own

        def columns(at):
            step = chips - at
            col_send[k, step] = jnp.dot(
                weights[...], cells[step], preferred_element_type=jnp.float32
            )
            col_copy(k, step).start()

        each(1, chips, columns)
        total = jnp.dot(weights[...], cells[0], preferred_element_type=jnp.float32)

        def add_columns(step, total):
            col_copy(k, step).wait_recv()
            return total + col_recv[k, step].astype(jnp.float32)

        total = lax.fori_loop(1, chips, add_columns, total)
        scale_v = observed_ref[...] / total
        if k < ITERS - 1:
            v_send[k] = scale_v.astype(jnp.bfloat16)
            v_recv[k, 0] = scale_v.astype(jnp.bfloat16)
        else:
            v_ref[...] = scale_v

    pred_copy.wait_send()
    predicted_copy.wait_send()
    for k in range(ITERS):
        row_copy(k).wait_send()

    def drain(step):
        obs_copy(step).wait_send()
        for k in range(ITERS):
            col_copy(k, step).wait_send()
        for k in range(ITERS - 1):
            v_copy(k, step).wait_send()

    each(1, chips, drain)


def on_device(chips, pred_points, obs_points, predicted, observed):
    coords, points = pred_points.shape
    freqs = predicted.shape[0]
    f32, bf16 = jnp.float32, jnp.bfloat16
    vmem = pl.BlockSpec(memory_space=pltpu.VMEM)
    cell_bytes = chips * 2 * points * points * 2
    pairs = chips * 2 * points * points
    scale_u, scale_v = pl.pallas_call(
        functools.partial(kernel, chips),
        out_shape=[jax.ShapeDtypeStruct((freqs, points), f32)] * 2,
        in_specs=[vmem] * 4,
        out_specs=[vmem] * 2,
        scratch_shapes=[
            pltpu.VMEM((chips, coords, points), f32),
            pltpu.VMEM((coords, points), f32),
            pltpu.VMEM((freqs, points), f32),
            pltpu.VMEM((2 * points, DEPTH), bf16),
            pltpu.VMEM((chips, 2 * points, points), bf16),
            pltpu.VMEM((2 * points, 128), f32),
            pltpu.VMEM((freqs, 2 * points), bf16),
            pltpu.VMEM((ITERS, chips, freqs, points), f32),
            pltpu.VMEM((ITERS, chips, freqs, points), f32),
            pltpu.VMEM((ITERS - 1, freqs, points), bf16),
            pltpu.VMEM((ITERS - 1, chips, freqs, points), bf16),
            pltpu.VMEM((ITERS, freqs, 2 * points), f32),
            pltpu.VMEM((ITERS, freqs, 2 * points), f32),
            pltpu.SemaphoreType.DMA((2, chips)),
            pltpu.SemaphoreType.DMA((2, ITERS, chips)),
            pltpu.SemaphoreType.DMA((2, ITERS - 1, chips)),
            pltpu.SemaphoreType.DMA((2, 2 + ITERS)),
        ],
        compiler_params=pltpu.CompilerParams(
            collective_id=0, has_side_effects=True,
            vmem_limit_bytes=cell_bytes + 24 * 2**20,
        ),
        cost_estimate=pl.CostEstimate(
            flops=pairs * (2 * DEPTH + 5 * 2 * freqs),
            bytes_accessed=4 * points * (2 * coords + 4 * freqs),
            transcendentals=pairs,
        ),
    )(pred_points, obs_points, predicted, observed)
    return jnp.log(scale_u), jnp.log(scale_v)


def solution(mesh):
    spec = P(None, ("batch", "row"))
    return jax.shard_map(
        functools.partial(on_device, mesh.shape["row"] // 2), mesh=mesh,
        in_specs=(spec,) * 4, out_specs=(spec,) * 2, check_vma=False,
    )
```

```python
import functools

import jax
import jax.numpy as jnp
from jax import lax
from jax.experimental import pallas as pl
from jax.experimental.pallas import tpu as pltpu
from jax.sharding import PartitionSpec as P

ITERS = 3
ENTROPY = 0.1
DEPTH = 64


def xor_index(left, right, bits):
    total = 0
    for bit in range(bits):
        unit = 1 << bit
        total = total + unit * ((left // unit + right // unit) % 2)
    return total


def three_parts(value):
    first = value.astype(jnp.bfloat16).astype(jnp.float32)
    rest = value - first
    second = rest.astype(jnp.bfloat16).astype(jnp.float32)
    return first, second, rest - second


def operand(points, is_source):
    centred = points - 0.5
    norm = jnp.sum(centred * centred, axis=0, keepdims=True) * (-1.0 / ENTROPY)
    n1, n2, n3 = three_parts(jnp.broadcast_to(norm, points.shape))
    row = lax.broadcasted_iota(jnp.int32, points.shape, 0)
    one, zero = jnp.ones_like(points), jnp.zeros_like(points)
    if is_source:
        a1, a2, a3 = three_parts(centred * (2.0 / ENTROPY))
        pieces = [a1, a1, a2, a2, a1, a3]
        n_first, one_first = 0, 3
    else:
        b1, b2, b3 = three_parts(centred)
        pieces = [b1, b2, b1, b2, b3, b1]
        n_first, one_first = 3, 0
    norms = jnp.where((row >= one_first) & (row < one_first + 3), one, zero)
    for place, part in enumerate((n1, n2, n3)):
        norms = jnp.where(row == n_first + place, part, norms)
    return jnp.concatenate(pieces + [norms, zero], axis=0)


def kernel(
    chips, pred_in, obs_in, predicted_in, observed_in, scale_ref,
    pred_ref, predicted_ref, observed_ref,
    obs_buf, pred_buf, predicted_buf, source, cells, acc, weights,
    first_send, first_recv, col_send, col_recv, known,
    v_send, v_recv, row_send, row_recv,
    in_sems, obs_sems, col_sems, v_sems, sib_sems,
):
    points = pred_ref.shape[1]
    freqs = predicted_ref.shape[0]
    me = lax.axis_index("row")
    core, chip = me % 2, me // 2
    sibling = {"row": me + 1 - 2 * core}
    bits = chips.bit_length() - 1
    power = chips == 1 << bits

    def ahead(step):
        other = xor_index(chip, step, bits) if power else (chip + step) % chips
        return {"row": other * 2 + core}

    def behind(step):
        other = xor_index(chip, step, bits) if power else (chip + chips - step) % chips
        return {"row": other * 2 + core}

    def remote(src, dst, sems, place, target):
        return pltpu.make_async_remote_copy(
            src_ref=src, dst_ref=dst, send_sem=sems.at[(0, *place)], recv_sem=sems.at[(1, *place)],
            device_id=target, device_id_type=pl.DeviceIdType.MESH,
        )

    def obs_copy(step):
        return remote(obs_buf.at[0], obs_buf.at[step], obs_sems, (step,), ahead(step))

    def col_copy(k, step):
        if k == 0:
            return remote(first_send.at[step], first_recv.at[step], col_sems, (k, step), behind(step))
        return remote(
            col_send.at[k - 1, step], col_recv.at[k - 1, step], col_sems, (k, step), behind(step))

    def v_copy(k, step):
        return remote(v_send.at[k], v_recv.at[k, step], v_sems, (k, step), ahead(step))

    def row_copy(k):
        return remote(row_send.at[k], row_recv.at[k], sib_sems, (2 + k,), sibling)

    pred_copy = remote(pred_ref, pred_buf, sib_sems, (0,), sibling)
    predicted_copy = remote(predicted_ref, predicted_buf, sib_sems, (1,), sibling)

    def each(first, last, act):
        lax.fori_loop(first, last, lambda at, _: (act(at), 0)[1], 0)

    fetches = [
        pltpu.make_async_copy(src, dst, in_sems.at[place])
        for place, (src, dst) in enumerate((
            (pred_in, pred_ref), (obs_in, obs_buf.at[0]),
            (predicted_in, predicted_ref), (observed_in, observed_ref),
        ))
    ]
    for fetch in fetches:
        fetch.start()
    barrier = pltpu.get_barrier_semaphore()
    pl.semaphore_signal(barrier, inc=1, device_id=sibling, device_id_type=pl.DeviceIdType.MESH)
    each(1, chips, lambda step: pl.semaphore_signal(
        barrier, inc=1, device_id=ahead(step), device_id_type=pl.DeviceIdType.MESH))
    acc[...] = jnp.zeros_like(acc)
    tile = min(256, points)

    def build(step, target, first_row, last_row):
        for first in range(first_row, last_row, tile):
            rows = slice(first, first + tile)
            exponent = jnp.dot(source[rows], target, preferred_element_type=jnp.float32)
            block = jnp.exp(exponent).astype(jnp.bfloat16)
            cells[step, rows] = block
            wide = block.astype(jnp.float32)
            sums = acc[rows]
            for lane in range(0, points, 128):
                sums = sums + wide[:, lane:lane + 128]
            acc[rows] = sums

    fetches[0].wait()
    source[:points] = operand(pred_ref[...], True).T.astype(jnp.bfloat16)
    fetches[1].wait()
    own_target = operand(obs_buf[0], False).astype(jnp.bfloat16)
    build(0, own_target, 0, points)
    pl.semaphore_wait(barrier, chips)

    pred_copy.start()
    each(1, chips, lambda at: obs_copy(chips - at).start())
    fetches[2].wait()
    predicted_copy.start()
    fetches[3].wait()
    pred_copy.wait_recv()
    source[points:] = operand(pred_buf[...], True).T.astype(jnp.bfloat16)
    build(0, own_target, points, 2 * points)

    def build_next(step):
        obs_copy(step).wait_recv()
        build(step, operand(obs_buf[step], False).astype(jnp.bfloat16), 0, 2 * points)

    each(1, chips, build_next)
    row_sums = jnp.sum(acc[...].T, axis=0, keepdims=True)
    row_send[0] = jnp.broadcast_to(row_sums, row_send.shape[1:])
    row_copy(0).start()
    predicted_copy.wait_recv()

    others = jnp.zeros((freqs, points), jnp.float32)
    for k in range(ITERS):
        if k > 0:
            each(1, chips, lambda at: v_copy(k - 1, chips - at).start())

            def add_rows(step, total):
                @pl.when(step > 0)
                def _():
                    v_copy(k - 1, step).wait_recv()

                return total + lax.dot_general(
                    v_recv[k - 1, step], cells[step], (((1,), (1,)), ((), ())),
                    preferred_element_type=jnp.float32,
                )

            row_send[k] = lax.fori_loop(
                0, chips, add_rows, jnp.zeros((freqs, 2 * points), jnp.float32))
            row_copy(k).start()
        row_copy(k).wait_recv()
        own = predicted_ref[...] / (row_send[k, :, :points] + row_recv[k, :, points:])
        other = predicted_buf[...] / (row_send[k, :, points:] + row_recv[k, :, :points])
        weights[:, :points] = own.astype(jnp.bfloat16)
        weights[:, points:] = other.astype(jnp.bfloat16)
        if k == ITERS - 1:
            scale_ref[0] = own

        def columns(at):
            step = chips - at
            sums = jnp.dot(weights[...], cells[step], preferred_element_type=jnp.float32)
            if k == 0:
                first_send[step] = sums
            else:
                before = first_send[step] if k == 1 else known[step]
                change = (sums - before).astype(jnp.bfloat16)
                col_send[k - 1, step] = change
                if k < ITERS - 1:
                    known[step] = before + change.astype(jnp.float32)
            col_copy(k, step).start()

        each(1, chips, columns)
        own_sums = jnp.dot(weights[...], cells[0], preferred_element_type=jnp.float32)

        def add_columns(step, total):
            col_copy(k, step).wait_recv()
            if k == 0:
                return total + first_recv[step]
            return total + col_recv[k - 1, step].astype(jnp.float32)

        others = lax.fori_loop(1, chips, add_columns, others)
        scale_v = observed_ref[...] / (own_sums + others)
        if k < ITERS - 1:
            v_send[k] = scale_v.astype(jnp.bfloat16)
            v_recv[k, 0] = scale_v.astype(jnp.bfloat16)
        else:
            scale_ref[1] = scale_v

    pred_copy.wait_send()
    predicted_copy.wait_send()
    for k in range(ITERS):
        row_copy(k).wait_send()

    def drain(step):
        obs_copy(step).wait_send()
        for k in range(ITERS):
            col_copy(k, step).wait_send()
        for k in range(ITERS - 1):
            v_copy(k, step).wait_send()

    each(1, chips, drain)


def on_device(chips, pred_points, obs_points, predicted, observed):
    coords, points = pred_points.shape
    freqs = predicted.shape[0]
    f32, bf16 = jnp.float32, jnp.bfloat16
    vmem = pl.BlockSpec(memory_space=pltpu.VMEM)
    cell_bytes = chips * 2 * points * points * 2
    pairs = chips * 2 * points * points
    scales = pl.pallas_call(
        functools.partial(kernel, chips),
        out_shape=jax.ShapeDtypeStruct((2, freqs, points), f32),
        in_specs=[pl.BlockSpec(memory_space=pltpu.HBM)] * 4,
        out_specs=vmem,
        scratch_shapes=[
            pltpu.VMEM((coords, points), f32),
            pltpu.VMEM((freqs, points), f32),
            pltpu.VMEM((freqs, points), f32),
            pltpu.VMEM((chips, coords, points), f32),
            pltpu.VMEM((coords, points), f32),
            pltpu.VMEM((freqs, points), f32),
            pltpu.VMEM((2 * points, DEPTH), bf16),
            pltpu.VMEM((chips, 2 * points, points), bf16),
            pltpu.VMEM((2 * points, 128), f32),
            pltpu.VMEM((freqs, 2 * points), bf16),
            pltpu.VMEM((chips, freqs, points), f32),
            pltpu.VMEM((chips, freqs, points), f32),
            pltpu.VMEM((ITERS - 1, chips, freqs, points), bf16),
            pltpu.VMEM((ITERS - 1, chips, freqs, points), bf16),
            pltpu.VMEM((chips, freqs, points), f32),
            pltpu.VMEM((ITERS - 1, freqs, points), bf16),
            pltpu.VMEM((ITERS - 1, chips, freqs, points), bf16),
            pltpu.VMEM((ITERS, freqs, 2 * points), f32),
            pltpu.VMEM((ITERS, freqs, 2 * points), f32),
            pltpu.SemaphoreType.DMA((4,)),
            pltpu.SemaphoreType.DMA((2, chips)),
            pltpu.SemaphoreType.DMA((2, ITERS, chips)),
            pltpu.SemaphoreType.DMA((2, ITERS - 1, chips)),
            pltpu.SemaphoreType.DMA((2, 2 + ITERS)),
        ],
        compiler_params=pltpu.CompilerParams(
            collective_id=0, has_side_effects=True,
            vmem_limit_bytes=cell_bytes + 24 * 2**20,
        ),
        cost_estimate=pl.CostEstimate(
            flops=pairs * (2 * DEPTH + 5 * 2 * freqs),
            bytes_accessed=4 * points * (2 * coords + 4 * freqs),
            transcendentals=pairs,
        ),
    )(pred_points, obs_points, predicted, observed)
    return jnp.log(scales[0]), jnp.log(scales[1])


def solution(mesh):
    spec = P(None, ("batch", "row"))
    return jax.shard_map(
        functools.partial(on_device, mesh.shape["row"] // 2), mesh=mesh,
        in_specs=(spec,) * 4, out_specs=(spec,) * 2, check_vma=False,
    )
```

```python
import functools

import jax
import jax.numpy as jnp
from jax import lax
from jax.experimental import pallas as pl
from jax.experimental.pallas import tpu as pltpu
from jax.sharding import PartitionSpec as P

ITERS = 3
ENTROPY = 0.1
DEPTH = 64


def xor_index(left, right, bits):
    total = 0
    for bit in range(bits):
        unit = 1 << bit
        total = total + unit * ((left // unit + right // unit) % 2)
    return total


def three_parts(value):
    first = value.astype(jnp.bfloat16).astype(jnp.float32)
    rest = value - first
    second = rest.astype(jnp.bfloat16).astype(jnp.float32)
    return first, second, rest - second


def operand(points, is_source):
    centred = points - 0.5
    norm = jnp.sum(centred * centred, axis=0, keepdims=True) * (-1.0 / ENTROPY)
    n1, n2, n3 = three_parts(jnp.broadcast_to(norm, points.shape))
    row = lax.broadcasted_iota(jnp.int32, points.shape, 0)
    one, zero = jnp.ones_like(points), jnp.zeros_like(points)
    if is_source:
        a1, a2, a3 = three_parts(centred * (2.0 / ENTROPY))
        pieces = [a1, a1, a2, a2, a1, a3]
        n_first, one_first = 0, 3
    else:
        b1, b2, b3 = three_parts(centred)
        pieces = [b1, b2, b1, b2, b3, b1]
        n_first, one_first = 3, 0
    norms = jnp.where((row >= one_first) & (row < one_first + 3), one, zero)
    for place, part in enumerate((n1, n2, n3)):
        norms = jnp.where(row == n_first + place, part, norms)
    return jnp.concatenate(pieces + [norms, zero], axis=0)


def kernel(
    chips, pred_in, obs_in, predicted_in, observed_in, scale_ref,
    pred_ref, predicted_ref, observed_ref,
    obs_buf, pred_buf, predicted_buf, source, cells, acc, weights,
    first_send, first_recv, col_send, col_recv, known,
    v_send, v_recv, row_send, row_recv,
    in_sems, obs_sems, col_sems, v_sems, sib_sems,
):
    points = pred_ref.shape[1]
    freqs = predicted_ref.shape[0]
    me = lax.axis_index("row")
    core, chip = me % 2, me // 2
    sibling = {"row": me + 1 - 2 * core}
    bits = chips.bit_length() - 1
    power = chips == 1 << bits

    def ahead(step):
        other = xor_index(chip, step, bits) if power else (chip + step) % chips
        return {"row": other * 2 + core}

    def behind(step):
        other = xor_index(chip, step, bits) if power else (chip + chips - step) % chips
        return {"row": other * 2 + core}

    def remote(src, dst, sems, place, target):
        return pltpu.make_async_remote_copy(
            src_ref=src, dst_ref=dst, send_sem=sems.at[(0, *place)], recv_sem=sems.at[(1, *place)],
            device_id=target, device_id_type=pl.DeviceIdType.MESH,
        )

    def obs_copy(step):
        return remote(obs_buf.at[0], obs_buf.at[step], obs_sems, (step,), ahead(step))

    def col_copy(k, step):
        if k == 0:
            return remote(first_send.at[step], first_recv.at[step], col_sems, (k, step), behind(step))
        return remote(
            col_send.at[k - 1, step], col_recv.at[k - 1, step], col_sems, (k, step), behind(step))

    def v_copy(k, step):
        return remote(v_send.at[k], v_recv.at[k, step], v_sems, (k, step), ahead(step))

    def row_copy(k):
        return remote(row_send.at[k], row_recv.at[k], sib_sems, (2 + k,), sibling)

    pred_copy = remote(pred_ref, pred_buf, sib_sems, (0,), sibling)
    predicted_copy = remote(predicted_ref, predicted_buf, sib_sems, (1,), sibling)

    def each(first, last, act):
        lax.fori_loop(first, last, lambda at, _: (act(at), 0)[1], 0)

    fetches = [
        pltpu.make_async_copy(src, dst, in_sems.at[place])
        for place, (src, dst) in enumerate((
            (pred_in, pred_ref), (obs_in, obs_buf.at[0]),
            (predicted_in, predicted_ref), (observed_in, observed_ref),
        ))
    ]
    for fetch in fetches:
        fetch.start()
    barrier = pltpu.get_barrier_semaphore()
    pl.semaphore_signal(barrier, inc=1, device_id=sibling, device_id_type=pl.DeviceIdType.MESH)
    each(1, chips, lambda step: pl.semaphore_signal(
        barrier, inc=1, device_id=ahead(step), device_id_type=pl.DeviceIdType.MESH))
    acc[...] = jnp.zeros_like(acc)
    tile = min(256, points)

    def build(step, target, first_row, last_row):
        for first in range(first_row, last_row, tile):
            rows = slice(first, first + tile)
            exponent = jnp.dot(source[rows], target, preferred_element_type=jnp.float32)
            block = jnp.exp(exponent).astype(jnp.bfloat16)
            cells[step, rows] = block
            wide = block.astype(jnp.float32)
            sums = acc[rows]
            for lane in range(0, points, 128):
                sums = sums + wide[:, lane:lane + 128]
            acc[rows] = sums

    fetches[0].wait()
    source[:points] = operand(pred_ref[...], True).T.astype(jnp.bfloat16)
    fetches[1].wait()
    own_target = operand(obs_buf[0], False).astype(jnp.bfloat16)
    build(0, own_target, 0, points)
    pl.semaphore_wait(barrier, chips)

    pred_copy.start()
    each(1, chips, lambda step: obs_copy(step).start())
    fetches[2].wait()
    predicted_copy.start()
    fetches[3].wait()
    pred_copy.wait_recv()
    source[points:] = operand(pred_buf[...], True).T.astype(jnp.bfloat16)
    build(0, own_target, points, 2 * points)

    def build_next(step):
        obs_copy(step).wait_recv()
        build(step, operand(obs_buf[step], False).astype(jnp.bfloat16), 0, 2 * points)

    each(1, chips, build_next)
    row_sums = jnp.sum(acc[...].T, axis=0, keepdims=True)
    row_send[0] = jnp.broadcast_to(row_sums, row_send.shape[1:])
    row_copy(0).start()
    predicted_copy.wait_recv()

    others = jnp.zeros((freqs, points), jnp.float32)
    for k in range(ITERS):
        if k > 0:
            each(1, chips, lambda step: v_copy(k - 1, step).start())

            def add_rows(step, total):
                @pl.when(step > 0)
                def _():
                    v_copy(k - 1, step).wait_recv()

                return total + lax.dot_general(
                    v_recv[k - 1, step], cells[step], (((1,), (1,)), ((), ())),
                    preferred_element_type=jnp.float32,
                )

            row_send[k] = lax.fori_loop(
                0, chips, add_rows, jnp.zeros((freqs, 2 * points), jnp.float32))
            row_copy(k).start()
        row_copy(k).wait_recv()
        own = predicted_ref[...] / (row_send[k, :, :points] + row_recv[k, :, points:])
        other = predicted_buf[...] / (row_send[k, :, points:] + row_recv[k, :, :points])
        weights[:, :points] = own.astype(jnp.bfloat16)
        weights[:, points:] = other.astype(jnp.bfloat16)
        if k == ITERS - 1:
            scale_ref[0] = own

        def columns(at):
            step = chips - at
            sums = jnp.dot(weights[...], cells[step], preferred_element_type=jnp.float32)
            if k == 0:
                first_send[step] = sums
            else:
                before = first_send[step] if k == 1 else known[step]
                change = (sums - before).astype(jnp.bfloat16)
                col_send[k - 1, step] = change
                if k < ITERS - 1:
                    known[step] = before + change.astype(jnp.float32)
            col_copy(k, step).start()

        each(1, chips, columns)
        own_sums = jnp.dot(weights[...], cells[0], preferred_element_type=jnp.float32)

        def add_columns(step, total):
            col_copy(k, step).wait_recv()
            if k == 0:
                return total + first_recv[step]
            return total + col_recv[k - 1, step].astype(jnp.float32)

        others = lax.fori_loop(1, chips, add_columns, others)
        scale_v = observed_ref[...] / (own_sums + others)
        if k < ITERS - 1:
            v_send[k] = scale_v.astype(jnp.bfloat16)
            v_recv[k, 0] = scale_v.astype(jnp.bfloat16)
        else:
            scale_ref[1] = scale_v

    pred_copy.wait_send()
    predicted_copy.wait_send()
    for k in range(ITERS):
        row_copy(k).wait_send()

    def drain(step):
        obs_copy(step).wait_send()
        for k in range(ITERS):
            col_copy(k, step).wait_send()
        for k in range(ITERS - 1):
            v_copy(k, step).wait_send()

    each(1, chips, drain)


def on_device(chips, pred_points, obs_points, predicted, observed):
    coords, points = pred_points.shape
    freqs = predicted.shape[0]
    f32, bf16 = jnp.float32, jnp.bfloat16
    vmem = pl.BlockSpec(memory_space=pltpu.VMEM)
    pairs = chips * 2 * points * points
    scales = pl.pallas_call(
        functools.partial(kernel, chips),
        out_shape=jax.ShapeDtypeStruct((2, freqs, points), f32),
        in_specs=[pl.BlockSpec(memory_space=pltpu.HBM)] * 4,
        out_specs=vmem,
        scratch_shapes=[
            pltpu.VMEM((coords, points), f32),
            pltpu.VMEM((freqs, points), f32),
            pltpu.VMEM((freqs, points), f32),
            pltpu.VMEM((chips, coords, points), f32),
            pltpu.VMEM((coords, points), f32),
            pltpu.VMEM((freqs, points), f32),
            pltpu.VMEM((2 * points, DEPTH), bf16),
            pltpu.VMEM((chips, 2 * points, points), bf16),
            pltpu.VMEM((2 * points, 128), f32),
            pltpu.VMEM((freqs, 2 * points), bf16),
            pltpu.VMEM((chips, freqs, points), f32),
            pltpu.VMEM((chips, freqs, points), f32),
            pltpu.VMEM((ITERS - 1, chips, freqs, points), bf16),
            pltpu.VMEM((ITERS - 1, chips, freqs, points), bf16),
            pltpu.VMEM((chips, freqs, points), f32),
            pltpu.VMEM((ITERS - 1, freqs, points), bf16),
            pltpu.VMEM((ITERS - 1, chips, freqs, points), bf16),
            pltpu.VMEM((ITERS, freqs, 2 * points), f32),
            pltpu.VMEM((ITERS, freqs, 2 * points), f32),
            pltpu.SemaphoreType.DMA((4,)),
            pltpu.SemaphoreType.DMA((2, chips)),
            pltpu.SemaphoreType.DMA((2, ITERS, chips)),
            pltpu.SemaphoreType.DMA((2, ITERS - 1, chips)),
            pltpu.SemaphoreType.DMA((2, 2 + ITERS)),
        ],
        compiler_params=pltpu.CompilerParams(
            collective_id=0, has_side_effects=True,
            vmem_limit_bytes=64 * 2**20,
        ),
        cost_estimate=pl.CostEstimate(
            flops=pairs * (2 * DEPTH + 5 * 2 * freqs),
            bytes_accessed=4 * points * (2 * coords + 4 * freqs),
            transcendentals=pairs,
        ),
    )(pred_points, obs_points, predicted, observed)
    return jnp.log(scales[0]), jnp.log(scales[1])


def solution(mesh):
    spec = P(None, ("batch", "row"))
    return jax.shard_map(
        functools.partial(on_device, mesh.shape["row"] // 2), mesh=mesh,
        in_specs=(spec,) * 4, out_specs=(spec,) * 2, check_vma=False,
    )
```

```python
import functools

import jax
import jax.numpy as jnp
from jax import lax
from jax.experimental import pallas as pl
from jax.experimental.pallas import tpu as pltpu
from jax.sharding import PartitionSpec as P

ITERS = 3
ENTROPY = 0.1
DEPTH = 64


def three_parts(value):
    first = value.astype(jnp.bfloat16).astype(jnp.float32)
    rest = value - first
    second = rest.astype(jnp.bfloat16).astype(jnp.float32)
    return first, second, rest - second


def operand(points, is_source):
    centred = points - 0.5
    norm = jnp.sum(centred * centred, axis=0, keepdims=True) * (-1.0 / ENTROPY)
    n1, n2, n3 = three_parts(jnp.broadcast_to(norm, points.shape))
    row = lax.broadcasted_iota(jnp.int32, points.shape, 0)
    one, zero = jnp.ones_like(points), jnp.zeros_like(points)
    if is_source:
        a1, a2, a3 = three_parts(centred * (2.0 / ENTROPY))
        pieces = [a1, a1, a2, a2, a1, a3]
        n_first, one_first = 0, 3
    else:
        b1, b2, b3 = three_parts(centred)
        pieces = [b1, b2, b1, b2, b3, b1]
        n_first, one_first = 3, 0
    norms = jnp.where((row >= one_first) & (row < one_first + 3), one, zero)
    for place, part in enumerate((n1, n2, n3)):
        norms = jnp.where(row == n_first + place, part, norms)
    return jnp.concatenate(pieces + [norms, zero], axis=0)


def kernel(
    chips, pred_in, obs_in, predicted_in, observed_in, scale_ref,
    pred_ref, predicted_ref, observed_ref,
    obs_buf, pred_buf, predicted_buf, source, source_t, cells, cells_t, acc, weights,
    first_send, first_recv, col_send, col_recv, known,
    v_send, v_recv, row_send, row_recv,
    in_sems, obs_sems, col_sems, v_sems, sib_sems,
):
    points = pred_ref.shape[1]
    freqs = predicted_ref.shape[0]
    me = lax.axis_index("row")
    core, chip = me % 2, me // 2
    sibling = {"row": me + 1 - 2 * core}
    bits = chips.bit_length() - 1
    power = chips == 1 << bits
    flips = [(1 << bit) * (1 - 2 * ((chip // (1 << bit)) % 2)) for bit in range(bits)]

    def partner(step, forward):
        if not isinstance(step, int):
            return sibling
        if power:
            other = chip + sum(flips[bit] for bit in range(bits) if step >> bit & 1)
        else:
            other = (chip + (step if forward else chips - step)) % chips
        return {"row": other * 2 + core}

    def ahead(step):
        return partner(step, True)

    def behind(step):
        return partner(step, False)

    def remote(src, dst, sems, place, target):
        return pltpu.make_async_remote_copy(
            src_ref=src, dst_ref=dst, send_sem=sems.at[(0, *place)], recv_sem=sems.at[(1, *place)],
            device_id=target, device_id_type=pl.DeviceIdType.MESH,
        )

    def obs_copy(step):
        return remote(obs_buf.at[0], obs_buf.at[step], obs_sems, (step,), ahead(step))

    def col_copy(k, step):
        if k == 0:
            return remote(first_send.at[step], first_recv.at[step], col_sems, (k, step), behind(step))
        return remote(
            col_send.at[k - 1, step], col_recv.at[k - 1, step], col_sems, (k, step), behind(step))

    def v_copy(k, step):
        return remote(v_send.at[k], v_recv.at[k, step], v_sems, (k, step), ahead(step))

    def row_copy(k):
        return remote(row_send.at[k], row_recv.at[k], sib_sems, (2 + k,), sibling)

    pred_copy = remote(pred_ref, pred_buf, sib_sems, (0,), sibling)
    predicted_copy = remote(predicted_ref, predicted_buf, sib_sems, (1,), sibling)

    def each(first, last, act):
        lax.fori_loop(first, last, lambda at, _: (act(at), 0)[1], 0)

    fetches = [
        pltpu.make_async_copy(src, dst, in_sems.at[place])
        for place, (src, dst) in enumerate((
            (pred_in, pred_ref), (obs_in, obs_buf.at[0]),
            (predicted_in, predicted_ref), (observed_in, observed_ref),
        ))
    ]
    for fetch in fetches:
        fetch.start()
    barrier = pltpu.get_barrier_semaphore()
    pl.semaphore_signal(barrier, inc=1, device_id=sibling, device_id_type=pl.DeviceIdType.MESH)
    for step in range(1, chips):
        pl.semaphore_signal(
            barrier, inc=1, device_id=ahead(step), device_id_type=pl.DeviceIdType.MESH)
    acc[...] = jnp.zeros_like(acc)
    tile = min(256, points)

    def build(step, target, first_row, last_row):
        for first in range(first_row, last_row, tile):
            rows = slice(first, first + tile)
            exponent = jnp.dot(source[rows], target, preferred_element_type=jnp.float32)
            block = jnp.exp(exponent).astype(jnp.bfloat16)
            cells[step, rows] = block
            wide = block.astype(jnp.float32)
            sums = acc[rows]
            for lane in range(0, points, 128):
                sums = sums + wide[:, lane:lane + 128]
            acc[rows] = sums

    fetches[0].wait()
    pred_operand = operand(pred_ref[...], True)
    source[:points] = pred_operand.T.astype(jnp.bfloat16)
    source_t[:, :points] = pred_operand.astype(jnp.bfloat16)
    fetches[1].wait()
    own_target = operand(obs_buf[0], False).astype(jnp.bfloat16)
    build(0, own_target, 0, points)
    pl.semaphore_wait(barrier, chips)

    pred_copy.start()
    for step in range(1, chips):
        obs_copy(step).start()
    fetches[2].wait()
    predicted_copy.start()
    fetches[3].wait()
    pred_copy.wait_recv()
    pred_operand = operand(pred_buf[...], True)
    source[points:] = pred_operand.T.astype(jnp.bfloat16)
    source_t[:, points:] = pred_operand.astype(jnp.bfloat16)
    build(0, own_target, points, 2 * points)

    def build_next(step):
        obs_copy(step).wait_recv()
        build(step, operand(obs_buf[step], False).astype(jnp.bfloat16), 0, 2 * points)

    each(1, chips, build_next)
    def build_transposed(step):
        target = operand(obs_buf[step], False).T.astype(jnp.bfloat16)
        for first in range(0, points, tile):
            exponent = jnp.dot(
                target[first:first + tile], source_t[...], preferred_element_type=jnp.float32)
            cells_t[step, first:first + tile] = jnp.exp(exponent).astype(jnp.bfloat16)

    row_sums = jnp.sum(acc[...].T, axis=0, keepdims=True)
    row_send[0] = jnp.broadcast_to(row_sums, row_send.shape[1:])
    row_copy(0).start()
    predicted_copy.wait_recv()

    others = jnp.zeros((freqs, points), jnp.float32)
    for k in range(ITERS):
        if k > 0:
            for step in range(1, chips):
                v_copy(k - 1, step).start()

            def add_rows(step, total):
                @pl.when(step > 0)
                def _():
                    v_copy(k - 1, step).wait_recv()

                return total + jnp.dot(
                    v_recv[k - 1, step], cells_t[step], preferred_element_type=jnp.float32)

            row_send[k] = lax.fori_loop(
                0, chips, add_rows, jnp.zeros((freqs, 2 * points), jnp.float32))
            row_copy(k).start()
        row_copy(k).wait_recv()
        own = predicted_ref[...] / (row_send[k, :, :points] + row_recv[k, :, points:])
        other = predicted_buf[...] / (row_send[k, :, points:] + row_recv[k, :, :points])
        weights[:, :points] = own.astype(jnp.bfloat16)
        weights[:, points:] = other.astype(jnp.bfloat16)
        if k == ITERS - 1:
            scale_ref[0] = own

        def columns(step):
            sums = jnp.dot(weights[...], cells[step], preferred_element_type=jnp.float32)
            if k == 0:
                first_send[step] = sums
            else:
                before = first_send[step] if k == 1 else known[step]
                change = (sums - before).astype(jnp.bfloat16)
                col_send[k - 1, step] = change
                if k < ITERS - 1:
                    known[step] = before + change.astype(jnp.float32)
            col_copy(k, step).start()

        for step in range(chips - 1, 0, -1):
            columns(step)
        own_sums = jnp.dot(weights[...], cells[0], preferred_element_type=jnp.float32)

        if k == 0:
            each(0, chips, build_transposed)

        def add_columns(step, total):
            col_copy(k, step).wait_recv()
            if k == 0:
                return total + first_recv[step]
            return total + col_recv[k - 1, step].astype(jnp.float32)

        others = lax.fori_loop(1, chips, add_columns, others)
        scale_v = observed_ref[...] / (own_sums + others)
        if k < ITERS - 1:
            v_send[k] = scale_v.astype(jnp.bfloat16)
            v_recv[k, 0] = scale_v.astype(jnp.bfloat16)
        else:
            scale_ref[1] = scale_v

    pred_copy.wait_send()
    predicted_copy.wait_send()
    for k in range(ITERS):
        row_copy(k).wait_send()

    def drain(step):
        obs_copy(step).wait_send()
        for k in range(ITERS):
            col_copy(k, step).wait_send()
        for k in range(ITERS - 1):
            v_copy(k, step).wait_send()

    each(1, chips, drain)


def on_device(chips, pred_points, obs_points, predicted, observed):
    coords, points = pred_points.shape
    freqs = predicted.shape[0]
    f32, bf16 = jnp.float32, jnp.bfloat16
    vmem = pl.BlockSpec(memory_space=pltpu.VMEM)
    pairs = chips * 2 * points * points
    scales = pl.pallas_call(
        functools.partial(kernel, chips),
        out_shape=jax.ShapeDtypeStruct((2, freqs, points), f32),
        in_specs=[pl.BlockSpec(memory_space=pltpu.HBM)] * 4,
        out_specs=vmem,
        scratch_shapes=[
            pltpu.VMEM((coords, points), f32),
            pltpu.VMEM((freqs, points), f32),
            pltpu.VMEM((freqs, points), f32),
            pltpu.VMEM((chips, coords, points), f32),
            pltpu.VMEM((coords, points), f32),
            pltpu.VMEM((freqs, points), f32),
            pltpu.VMEM((2 * points, DEPTH), bf16),
            pltpu.VMEM((DEPTH, 2 * points), bf16),
            pltpu.VMEM((chips, 2 * points, points), bf16),
            pltpu.VMEM((chips, points, 2 * points), bf16),
            pltpu.VMEM((2 * points, 128), f32),
            pltpu.VMEM((freqs, 2 * points), bf16),
            pltpu.VMEM((chips, freqs, points), f32),
            pltpu.VMEM((chips, freqs, points), f32),
            pltpu.VMEM((ITERS - 1, chips, freqs, points), bf16),
            pltpu.VMEM((ITERS - 1, chips, freqs, points), bf16),
            pltpu.VMEM((chips, freqs, points), f32),
            pltpu.VMEM((ITERS - 1, freqs, points), bf16),
            pltpu.VMEM((ITERS - 1, chips, freqs, points), bf16),
            pltpu.VMEM((ITERS, freqs, 2 * points), f32),
            pltpu.VMEM((ITERS, freqs, 2 * points), f32),
            pltpu.SemaphoreType.DMA((4,)),
            pltpu.SemaphoreType.DMA((2, chips)),
            pltpu.SemaphoreType.DMA((2, ITERS, chips)),
            pltpu.SemaphoreType.DMA((2, ITERS - 1, chips)),
            pltpu.SemaphoreType.DMA((2, 2 + ITERS)),
        ],
        compiler_params=pltpu.CompilerParams(
            collective_id=0, has_side_effects=True,
            vmem_limit_bytes=64 * 2**20,
        ),
        cost_estimate=pl.CostEstimate(
            flops=pairs * (4 * DEPTH + 5 * 2 * freqs),
            bytes_accessed=4 * points * (2 * coords + 4 * freqs),
            transcendentals=2 * pairs,
        ),
    )(pred_points, obs_points, predicted, observed)
    return jnp.log(scales[0]), jnp.log(scales[1])


def solution(mesh):
    spec = P(None, ("batch", "row"))
    return jax.shard_map(
        functools.partial(on_device, mesh.shape["row"] // 2), mesh=mesh,
        in_specs=(spec,) * 4, out_specs=(spec,) * 2, check_vma=False,
    )
```

```python
import functools

import jax
import jax.numpy as jnp
from jax import lax
from jax.experimental import pallas as pl
from jax.experimental.pallas import tpu as pltpu
from jax.sharding import PartitionSpec as P

ITERS = 3
ENTROPY = 0.1
DEPTH = 64


def three_parts(value):
    first = value.astype(jnp.bfloat16).astype(jnp.float32)
    rest = value - first
    second = rest.astype(jnp.bfloat16).astype(jnp.float32)
    return first, second, rest - second


def operand(points, is_source):
    centred = points - 0.5
    norm = jnp.sum(centred * centred, axis=0, keepdims=True) * (-1.0 / ENTROPY)
    n1, n2, n3 = three_parts(jnp.broadcast_to(norm, points.shape))
    row = lax.broadcasted_iota(jnp.int32, points.shape, 0)
    one, zero = jnp.ones_like(points), jnp.zeros_like(points)
    if is_source:
        a1, a2, a3 = three_parts(centred * (2.0 / ENTROPY))
        pieces = [a1, a1, a2, a2, a1, a3]
        n_first, one_first = 0, 3
    else:
        b1, b2, b3 = three_parts(centred)
        pieces = [b1, b2, b1, b2, b3, b1]
        n_first, one_first = 3, 0
    norms = jnp.where((row >= one_first) & (row < one_first + 3), one, zero)
    for place, part in enumerate((n1, n2, n3)):
        norms = jnp.where(row == n_first + place, part, norms)
    return jnp.concatenate(pieces + [norms, zero], axis=0)


def kernel(
    chips, pred_in, obs_in, predicted_in, observed_in, scale_ref,
    pred_ref, predicted_ref, observed_ref,
    obs_buf, pred_buf, predicted_buf, source, source_t, cells, cells_t, acc, weights,
    first_send, first_recv, col_send, col_recv, known,
    v_send, v_recv, row_send, row_recv,
    in_sems, obs_sems, col_sems, v_sems, sib_sems,
):
    points = pred_ref.shape[1]
    freqs = predicted_ref.shape[0]
    me = lax.axis_index("row")
    core, chip = me % 2, me // 2
    sibling = {"row": me + 1 - 2 * core}
    bits = chips.bit_length() - 1
    power = chips == 1 << bits
    flips = [(1 << bit) * (1 - 2 * ((chip // (1 << bit)) % 2)) for bit in range(bits)]

    def partner(step, forward):
        if not isinstance(step, int):
            return sibling
        if power:
            other = chip + sum(flips[bit] for bit in range(bits) if step >> bit & 1)
        else:
            other = (chip + (step if forward else chips - step)) % chips
        return {"row": other * 2 + core}

    def ahead(step):
        return partner(step, True)

    def behind(step):
        return partner(step, False)

    def remote(src, dst, sems, place, target):
        return pltpu.make_async_remote_copy(
            src_ref=src, dst_ref=dst, send_sem=sems.at[(0, *place)], recv_sem=sems.at[(1, *place)],
            device_id=target, device_id_type=pl.DeviceIdType.MESH,
        )

    def obs_copy(step):
        return remote(obs_buf.at[0], obs_buf.at[step], obs_sems, (step,), ahead(step))

    def col_copy(k, step):
        if k == 0:
            return remote(first_send.at[step], first_recv.at[step], col_sems, (k, step), behind(step))
        return remote(
            col_send.at[k - 1, step], col_recv.at[k - 1, step], col_sems, (k, step), behind(step))

    def v_copy(k, step):
        return remote(v_send.at[k], v_recv.at[k, step], v_sems, (k, step), ahead(step))

    def row_copy(k):
        return remote(row_send.at[k], row_recv.at[k], sib_sems, (2 + k,), sibling)

    pred_copy = remote(pred_ref, pred_buf, sib_sems, (0,), sibling)
    predicted_copy = remote(predicted_ref, predicted_buf, sib_sems, (1,), sibling)

    def each(first, last, act):
        lax.fori_loop(first, last, lambda at, _: (act(at), 0)[1], 0)

    fetches = [
        pltpu.make_async_copy(src, dst, in_sems.at[place])
        for place, (src, dst) in enumerate((
            (pred_in, pred_ref), (obs_in, obs_buf.at[0]),
            (predicted_in, predicted_ref), (observed_in, observed_ref),
        ))
    ]
    for fetch in fetches:
        fetch.start()
    barrier = pltpu.get_barrier_semaphore()
    pl.semaphore_signal(barrier, inc=1, device_id=sibling, device_id_type=pl.DeviceIdType.MESH)
    for step in range(1, chips):
        pl.semaphore_signal(
            barrier, inc=1, device_id=ahead(step), device_id_type=pl.DeviceIdType.MESH)
    acc[...] = jnp.zeros_like(acc)
    tile = min(256, points)

    def build(step, target, first_row, last_row):
        for first in range(first_row, last_row, tile):
            rows = slice(first, first + tile)
            exponent = jnp.dot(source[rows], target, preferred_element_type=jnp.float32)
            block = jnp.exp(exponent).astype(jnp.bfloat16)
            cells[step, rows] = block
            wide = block.astype(jnp.float32)
            sums = acc[rows]
            for lane in range(0, points, 128):
                sums = sums + wide[:, lane:lane + 128]
            acc[rows] = sums

    fetches[0].wait()
    pred_operand = operand(pred_ref[...], True)
    source[:points] = pred_operand.T.astype(jnp.bfloat16)
    source_t[:, :points] = pred_operand.astype(jnp.bfloat16)
    fetches[1].wait()
    own_target = operand(obs_buf[0], False).astype(jnp.bfloat16)
    pl.semaphore_wait(barrier, chips)

    pred_copy.start()
    for step in range(1, chips):
        obs_copy(step).start()
    fetches[2].wait()
    predicted_copy.start()
    fetches[3].wait()
    build(0, own_target, 0, points)
    pred_copy.wait_recv()
    pred_operand = operand(pred_buf[...], True)
    source[points:] = pred_operand.T.astype(jnp.bfloat16)
    source_t[:, points:] = pred_operand.astype(jnp.bfloat16)
    build(0, own_target, points, 2 * points)

    def build_next(step):
        obs_copy(step).wait_recv()
        build(step, operand(obs_buf[step], False).astype(jnp.bfloat16), 0, 2 * points)

    each(1, chips, build_next)
    def build_transposed(step):
        target = operand(obs_buf[step], False).T.astype(jnp.bfloat16)
        for first in range(0, points, tile):
            exponent = jnp.dot(
                target[first:first + tile], source_t[...], preferred_element_type=jnp.float32)
            cells_t[step, first:first + tile] = jnp.exp(exponent).astype(jnp.bfloat16)

    row_sums = jnp.sum(acc[...].T, axis=0, keepdims=True)
    row_send[0] = jnp.broadcast_to(row_sums, row_send.shape[1:])
    row_copy(0).start()
    predicted_copy.wait_recv()

    others = jnp.zeros((freqs, points), jnp.float32)
    for k in range(ITERS):
        if k > 0:
            for step in range(chips - 1, 0, -1):
                v_copy(k - 1, step).start()

            def add_rows(step, total):
                if step > 0:
                    v_copy(k - 1, step).wait_recv()
                return total + jnp.dot(
                    v_recv[k - 1, step], cells_t[step], preferred_element_type=jnp.float32)

            products = jnp.zeros((freqs, 2 * points), jnp.float32)
            for step in range(chips):
                products = add_rows(step, products)
            row_send[k] = products
            row_copy(k).start()
        row_copy(k).wait_recv()
        own = predicted_ref[...] / (row_send[k, :, :points] + row_recv[k, :, points:])
        other = predicted_buf[...] / (row_send[k, :, points:] + row_recv[k, :, :points])
        weights[:, :points] = own.astype(jnp.bfloat16)
        weights[:, points:] = other.astype(jnp.bfloat16)
        if k == ITERS - 1:
            scale_ref[0] = own

        def columns(step):
            sums = jnp.dot(weights[...], cells[step], preferred_element_type=jnp.float32)
            if k == 0:
                first_send[step] = sums
            else:
                before = first_send[step] if k == 1 else known[step]
                change = (sums - before).astype(jnp.bfloat16)
                col_send[k - 1, step] = change
                if k < ITERS - 1:
                    known[step] = before + change.astype(jnp.float32)
            col_copy(k, step).start()

        for step in range(chips - 1, 0, -1):
            columns(step)
        own_sums = jnp.dot(weights[...], cells[0], preferred_element_type=jnp.float32)

        if k == 0:
            each(0, chips, build_transposed)

        def add_columns(step, total):
            col_copy(k, step).wait_recv()
            if k == 0:
                return total + first_recv[step]
            return total + col_recv[k - 1, step].astype(jnp.float32)

        for step in range(1, chips):
            others = add_columns(step, others)
        scale_v = observed_ref[...] / (own_sums + others)
        if k < ITERS - 1:
            v_send[k] = scale_v.astype(jnp.bfloat16)
            v_recv[k, 0] = scale_v.astype(jnp.bfloat16)
        else:
            scale_ref[1] = scale_v

    pred_copy.wait_send()
    predicted_copy.wait_send()
    for k in range(ITERS):
        row_copy(k).wait_send()

    def drain(step):
        obs_copy(step).wait_send()
        for k in range(ITERS):
            col_copy(k, step).wait_send()
        for k in range(ITERS - 1):
            v_copy(k, step).wait_send()

    each(1, chips, drain)


def on_device(chips, pred_points, obs_points, predicted, observed):
    coords, points = pred_points.shape
    freqs = predicted.shape[0]
    f32, bf16 = jnp.float32, jnp.bfloat16
    vmem = pl.BlockSpec(memory_space=pltpu.VMEM)
    pairs = chips * 2 * points * points
    scales = pl.pallas_call(
        functools.partial(kernel, chips),
        out_shape=jax.ShapeDtypeStruct((2, freqs, points), f32),
        in_specs=[pl.BlockSpec(memory_space=pltpu.HBM)] * 4,
        out_specs=vmem,
        scratch_shapes=[
            pltpu.VMEM((coords, points), f32),
            pltpu.VMEM((freqs, points), f32),
            pltpu.VMEM((freqs, points), f32),
            pltpu.VMEM((chips, coords, points), f32),
            pltpu.VMEM((coords, points), f32),
            pltpu.VMEM((freqs, points), f32),
            pltpu.VMEM((2 * points, DEPTH), bf16),
            pltpu.VMEM((DEPTH, 2 * points), bf16),
            pltpu.VMEM((chips, 2 * points, points), bf16),
            pltpu.VMEM((chips, points, 2 * points), bf16),
            pltpu.VMEM((2 * points, 128), f32),
            pltpu.VMEM((freqs, 2 * points), bf16),
            pltpu.VMEM((chips, freqs, points), f32),
            pltpu.VMEM((chips, freqs, points), f32),
            pltpu.VMEM((ITERS - 1, chips, freqs, points), bf16),
            pltpu.VMEM((ITERS - 1, chips, freqs, points), bf16),
            pltpu.VMEM((chips, freqs, points), f32),
            pltpu.VMEM((ITERS - 1, freqs, points), bf16),
            pltpu.VMEM((ITERS - 1, chips, freqs, points), bf16),
            pltpu.VMEM((ITERS, freqs, 2 * points), f32),
            pltpu.VMEM((ITERS, freqs, 2 * points), f32),
            pltpu.SemaphoreType.DMA((4,)),
            pltpu.SemaphoreType.DMA((2, chips)),
            pltpu.SemaphoreType.DMA((2, ITERS, chips)),
            pltpu.SemaphoreType.DMA((2, ITERS - 1, chips)),
            pltpu.SemaphoreType.DMA((2, 2 + ITERS)),
        ],
        compiler_params=pltpu.CompilerParams(
            collective_id=0, has_side_effects=True,
            vmem_limit_bytes=64 * 2**20,
        ),
        cost_estimate=pl.CostEstimate(
            flops=pairs * (4 * DEPTH + 5 * 2 * freqs),
            bytes_accessed=4 * points * (2 * coords + 4 * freqs),
            transcendentals=2 * pairs,
        ),
    )(pred_points, obs_points, predicted, observed)
    return jnp.log(scales[0]), jnp.log(scales[1])


def solution(mesh):
    spec = P(None, ("batch", "row"))
    return jax.shard_map(
        functools.partial(on_device, mesh.shape["row"] // 2), mesh=mesh,
        in_specs=(spec,) * 4, out_specs=(spec,) * 2, check_vma=False,
    )
```
